32 devices in a mesh: groups: 2 (over x), seg: 16 (over z, y, core).
Axes of the slice: x: 2, y: 2, z: 4, core: 2. Of those that a mesh axis runs over, the one named last changes fastest.
Arguments:
- psi_start: float32 [32, 1, 256, 256], P(('groups', 'seg')), parts along dimension 0, may hold values from -400 to 400
- block_sizes: int32 [32, 1, 2], P(('groups', 'seg')), parts along dimension 0, may hold values from 42 to 256, as said below
- environment: bfloat16 [32, 2, 1, 34, 256, 256], P(('groups', 'seg')), parts along dimension 0, may hold values from -3 to 3, as said below
Outputs:
- wavefunction: float32 [32, 1, 256, 256], P(('groups', 'seg')), parts along dimension 0
- energies: float32 [32, 2], P(('groups', 'seg')), parts along dimension 0
- sweep_energy: float32 [4], P('groups'), parts along dimension 0
The draws below stay inside these ranges and needn't reach their ends.
There are 2 independent parts, one for each index of `groups`. The reference program is written for one: setup_inputs(seed, part) draws one part's arguments, and reference() takes and returns one part's arrays. A program takes and returns all parts, laid end to end along the dimension named above; each array names one. Nothing has to cross between parts.
Inputs may be any that keep to these rules, and one draw needn't show every extreme that they name: `block_sizes`: live left and right states of a sector block; in every draw some block has 256 of both. Every matrix environment[d, e, s, k] is symmetric.
All inputs are finite; a program needn't handle non-finite values.
Results may differ from the reference program's by a relative error of at most 0.0045.
Values may be sent and summed in bfloat16 or wider, within the bound.
A program may use at most 128 MiB of HBM per device.

```python
import math
import jax
import jax.numpy as jnp
from jax import lax

B = 256
K = 34
S = 1
ITERS = 2
N_SEG = 16


def draw_environment(key, part):
    key = jax.random.fold_in(key, 11)
    eye_band = (lax.iota(jnp.int32, B)[:, None] == lax.iota(jnp.int32, B)[None, :]).astype(jnp.float32)

    def one_device(device_index):
        dev_key = jax.random.fold_in(key, device_index)
        noise_key, diag_key = jax.random.split(dev_key)
        noise_draw = jnp.clip(jax.random.normal(noise_key, (2, S, K, B, B), jnp.float32), -4.0, 4.0)
        symmetric = (noise_draw + jnp.swapaxes(noise_draw, -1, -2)) * math.sqrt(0.5 / B)
        diag_values = jax.random.uniform(diag_key, (2, S, K, B), jnp.float32, -1.5, 1.5)
        return (symmetric + eye_band * diag_values[..., None]).astype(jnp.bfloat16)
    return lax.map(one_device, jnp.arange(N_SEG, dtype=jnp.int32))


def draw_psi_start(key, part):
    key = jax.random.fold_in(key, 12)
    base_key, row_key, col_key = jax.random.split(key, 3)
    field_shape = (N_SEG, S, B, B)
    base_draw = jnp.clip(jax.random.normal(base_key, field_shape, jnp.float32), -4.0, 4.0)
    spread = math.log(10.0)
    row_scale = jnp.exp(jax.random.uniform(row_key, (N_SEG, S, B, 1), jnp.float32, 0.0, spread))
    col_scale = jnp.exp(jax.random.uniform(col_key, (N_SEG, S, 1, B), jnp.float32, 0.0, spread))
    return base_draw * row_scale * col_scale


def draw_block_sizes(key, part):
    key = jax.random.fold_in(key, 13)
    size_key, pick_key = jax.random.split(key)
    drawn = jax.random.randint(size_key, (N_SEG, S, 2), max(B // 6, 1), B + 1, dtype=jnp.int32)
    chosen = jax.random.randint(pick_key, (), 0, N_SEG * S, dtype=jnp.int32)
    flat_index = lax.iota(jnp.int32, N_SEG * S).reshape(N_SEG, S, 1)
    return jnp.where(flat_index == chosen, B, drawn).astype(jnp.int32)


def setup_inputs(seed: int = 0, part: int = 0) -> dict:
    splits = jax.random.split(jax.random.key(seed), 4)
    part_splits = jax.random.split(jax.random.fold_in(splits[3], part), 4)
    psi_start = draw_psi_start(jax.random.fold_in(jax.random.fold_in(splits[3], part), 71), part)
    block_sizes = draw_block_sizes(jax.random.fold_in(jax.random.fold_in(splits[3], part), 71), part)
    environment = draw_environment(jax.random.fold_in(jax.random.fold_in(splits[3], part), 71), part)
    return dict(psi_start=psi_start, block_sizes=block_sizes, environment=environment)


EPSILON = 1e-06
PRECISE = lax.Precision.HIGHEST

def rounded(values):
    return lax.optimization_barrier(values.astype(jnp.bfloat16)).astype(jnp.float32)

def ritz_pair(rayleigh, coupling, curvature):
    half_gap = 0.5 * (rayleigh - curvature)
    energy_now = 0.5 * (rayleigh + curvature) - jnp.sqrt(half_gap * half_gap + coupling * coupling)
    weight_old = curvature - energy_now
    weight_new = -coupling
    length_pair = jnp.sqrt(weight_old * weight_old + weight_new * weight_new)
    return (energy_now, weight_old / length_pair, weight_new / length_pair)

def reference(psi_start, block_sizes, environment):
    bonds = N_SEG // 2
    grouped = environment.reshape(bonds, 2, 2, S, K, B, B)
    left_even = grouped[:, 0, 0]
    right_even = grouped[:, 1, 1]
    left_odd = grouped[:, 0, 1]
    right_odd = grouped[:, 1, 0]
    initial = psi_start.reshape(bonds, 2, S, B, B)
    dims = block_sizes.reshape(bonds, 2, S, 2)
    positions = jnp.arange(B, dtype=jnp.int32)
    row_live = positions[:, None] < dims[..., 0, None, None]
    col_live = positions[None, :] < dims[..., 1, None, None]
    live_mask = (row_live & col_live).astype(jnp.float32)

    def one_bond(inputs):
        left_e, right_e, left_o, right_o, start_pair, mask_pair = inputs
        left_e = left_e.astype(jnp.float32)
        right_e = right_e.astype(jnp.float32)
        left_o = left_o.astype(jnp.float32)
        right_o = right_o.astype(jnp.float32)

        def apply_operator(state):
            lowered = rounded(state)
            even_part = rounded(jnp.einsum('skij,sjl->skil', left_e, lowered[0], precision=PRECISE))
            even_image = jnp.einsum('skil,sklm->sim', even_part, right_e, precision=PRECISE)
            odd_part = rounded(jnp.einsum('sij,skjl->skil', lowered[1], right_o, precision=PRECISE))
            odd_image = jnp.einsum('skij,skjl->sil', left_o, odd_part, precision=PRECISE)
            return jnp.stack([even_image, odd_image]) * mask_pair
        diag_even = jnp.einsum('ski,skj->sij', jnp.diagonal(left_e, axis1=-2, axis2=-1), jnp.diagonal(right_e, axis1=-2, axis2=-1), precision=PRECISE)
        diag_odd = jnp.einsum('ski,skj->sij', jnp.diagonal(left_o, axis1=-2, axis2=-1), jnp.diagonal(right_o, axis1=-2, axis2=-1), precision=PRECISE)
        precondition = jnp.stack([diag_even, diag_odd])
        vector = start_pair * mask_pair
        vector = vector / jnp.sqrt(jnp.sum(vector * vector) + EPSILON)
        image = apply_operator(vector)
        energy_list = []
        for iteration in range(ITERS):
            rayleigh = jnp.sum(vector * image)
            correction = (image - rayleigh * vector) / jnp.maximum(jnp.abs(precondition - rayleigh), 1.0)
            correlation = jnp.sum(vector * correction)
            correction = correction - correlation * vector
            correction = correction / jnp.sqrt(jnp.sum(correction * correction) + EPSILON)
            corr_image = apply_operator(correction)
            coupling = jnp.sum(vector * corr_image)
            curvature = jnp.sum(correction * corr_image)
            energy_now, weight_old, weight_new = ritz_pair(rayleigh, coupling, curvature)
            vector = weight_old * vector + weight_new * correction
            image = weight_old * image + weight_new * corr_image
            energy_list.append(energy_now)
        return (vector * B, jnp.stack(energy_list))
    wave, energy = lax.map(one_bond, (left_even, right_even, left_odd, right_odd, initial, live_mask))
    bond_weight = 1.0 + 2.0 * jnp.arange(bonds, dtype=jnp.float32) / float(max(bonds - 1, 1))
    sweep_energy = lax.optimization_barrier(jnp.sum(bond_weight[:, None] * energy, axis=0)) / float(bonds)
    return (wave.reshape(N_SEG, S, B, B), jnp.repeat(energy, 2, axis=0), sweep_energy)
```

```python
import functools

import jax
import jax.numpy as jnp
from jax import lax
from jax.experimental import pallas as pl
from jax.experimental.pallas import tpu as pltpu
from jax.sharding import PartitionSpec as P

ITERS = 2
EPSILON = 1e-06
F32 = jnp.float32
BF16 = jnp.bfloat16


def ritz_pair(rayleigh, coupling, curvature):
    half_gap = 0.5 * (rayleigh - curvature)
    energy_now = 0.5 * (rayleigh + curvature) - jnp.sqrt(half_gap * half_gap + coupling * coupling)
    weight_old = curvature - energy_now
    weight_new = -coupling
    length_pair = jnp.sqrt(weight_old * weight_old + weight_new * weight_new)
    return energy_now, weight_old / length_pair, weight_new / length_pair


def project(vv, rayleigh, vc, cc, vh, ch, ci):
    squared = jnp.maximum(cc - vc * vc * (2.0 - vv), 0.0)
    inv = 1.0 / jnp.sqrt(squared + EPSILON)
    coupling = (vh - vc * rayleigh) * inv
    mirrored = (ci - vc * rayleigh) * inv
    curvature = (ch - vc * (ci + vh) + vc * vc * rayleigh) * (inv * inv)
    energy, old, new = ritz_pair(rayleigh, coupling, curvature)
    scale_c = new * inv
    scale_v = old - scale_c * vc
    next_rayleigh = old * old * rayleigh + old * new * (coupling + mirrored) + new * new * curvature
    next_vv = scale_v * scale_v * vv + 2.0 * scale_v * scale_c * vc + scale_c * scale_c * cc
    return energy, scale_v, scale_c, next_rayleigh, next_vv


def rows_of(*fields):
    rows = []
    for field in fields:
        if field.shape[0] > 1:
            field = jnp.sum(field, axis=0, keepdims=True)
        half = field.shape[1] // 128
        total = field[:, :128]
        for part in range(1, half):
            total = total + field[:, part * 128:(part + 1) * 128]
        rows.append(total)
    rows.append(jnp.zeros((8 - len(rows), 128), F32))
    stacked = jnp.concatenate(rows, axis=0)
    return jnp.broadcast_to(jnp.sum(stacked, axis=1, keepdims=True), (8, 128))


def kernel(
    n, chunk, psi_ref, sizes_ref, env_ref, wave_ref, energies_ref, sweep_ref,
    psi, own, other, parts, acc, diag_own, diag_other, stats, stats_in, gathered,
    psi_sem, own_sem, send_sem, recv_sem, stat_send, stat_recv, all_send, all_recv,
):
    channels, size = own.shape[0], own.shape[1]
    half = size // 2
    chunks = channels // chunk
    me = lax.axis_index("seg")
    parity = lax.rem(me, 2)
    partner = me + 1 - 2 * parity
    bond = lax.div(me, 2)
    odd = parity == 1

    barrier = pltpu.get_barrier_semaphore()
    for step in range(1, n):
        pl.semaphore_signal(
            barrier, inc=1, device_id={"seg": lax.rem(me + step, n)}, device_id_type=pl.DeviceIdType.MESH
        )
    psi_copy = pltpu.make_async_copy(psi_ref.at[0, 0], psi, psi_sem)
    psi_copy.start()
    own_copies = []
    for c in range(chunks):
        copy = pltpu.make_async_copy(
            env_ref.at[0, 0, 0, pl.ds(c * chunk, chunk)], own.at[pl.ds(c * chunk, chunk)], own_sem.at[c]
        )
        copy.start()
        own_copies.append(copy)
    pl.semaphore_wait(barrier, n - 1)

    def to_partner(src, dst, sent, received):
        copy = pltpu.make_async_remote_copy(
            src_ref=src, dst_ref=dst, send_sem=sent, recv_sem=received,
            device_id={"seg": partner}, device_id_type=pl.DeviceIdType.MESH,
        )
        copy.start()
        return copy

    sends = []
    for c in range(chunks):
        ks = pl.ds(c * chunk, chunk)
        sends.append((
            to_partner(
                env_ref.at[0, 1, 0, ks, pl.ds(0, half)], other.at[ks, pl.ds(0, half)],
                send_sem.at[2 * c], recv_sem.at[2 * c],
            ),
            to_partner(
                env_ref.at[0, 1, 0, ks, pl.ds(half, half), pl.ds(half, half)],
                other.at[ks, pl.ds(half, half), pl.ds(half, half)],
                send_sem.at[2 * c + 1], recv_sem.at[2 * c + 1],
            ),
        ))

    row_at = lax.broadcasted_iota(jnp.int32, (size, size), 0)
    col_at = lax.broadcasted_iota(jnp.int32, (size, size), 1)
    dim0, dim1 = sizes_ref[0, 0, 0], sizes_ref[0, 0, 1]
    row_size = jnp.where(odd, dim1, dim0)
    col_size = jnp.where(odd, dim0, dim1)

    def masked(field):
        return jnp.where((row_at < row_size) & (col_at < col_size), field, 0.0)

    def wide(row):
        return jnp.concatenate([row] * (size // 128), axis=1)

    eye = (
        lax.broadcasted_iota(jnp.int32, (half, half), 0) == lax.broadcasted_iota(jnp.int32, (half, half), 1)
    )

    def diagonals(ref, out, k):
        low = jnp.where(eye, ref[k, 0:half, 0:half].astype(F32), 0.0)
        high = jnp.where(eye, ref[k, half:size, half:size].astype(F32), 0.0)
        out[k:k + 1, 0:half] = jnp.sum(low, axis=0, keepdims=True)
        out[k:k + 1, half:size] = jnp.sum(high, axis=0, keepdims=True)

    diag_own[...] = jnp.zeros_like(diag_own)
    diag_other[...] = jnp.zeros_like(diag_other)

    psi_copy.wait()

    @pl.when(odd)
    def _():
        psi[...] = psi[...].T

    start = masked(psi[...])
    psi[...] = start
    lowered = start.astype(BF16)
    for c in range(chunks):
        own_copies[c].wait()
        for k in range(c * chunk, (c + 1) * chunk):
            parts[:, k * size:(k + 1) * size] = jnp.dot(
                own[k], lowered, preferred_element_type=F32
            ).astype(BF16)
            diagonals(own, diag_own, k)

    for c in range(chunks):
        for copy in sends[c]:
            copy.wait_recv()
        for k in range(c * chunk, (c + 1) * chunk):
            other[k, half:size, 0:half] = other[k, 0:half, half:size].T
            diagonals(other, diag_other, k)
        ks = slice(c * chunk * size, (c + 1) * chunk * size)
        product = jnp.dot(
            parts[:, ks],
            other[c * chunk:(c + 1) * chunk].reshape(chunk * size, size),
            preferred_element_type=F32,
        )
        acc[...] = product if c == 0 else acc[...] + product

    def apply_operator(field):
        low = field.astype(BF16)
        for k in range(channels):
            parts[:, k * size:(k + 1) * size] = jnp.dot(
                own[k], low, preferred_element_type=F32
            ).astype(BF16)
        return masked(jnp.dot(
            parts[...], other[...].reshape(channels * size, size), preferred_element_type=F32
        ))

    start = psi[...]
    image = masked(acc[...])
    stats[0] = rows_of(start * start, start * image)
    stat_copy = to_partner(stats.at[0], stats_in.at[0], stat_send.at[0], stat_recv.at[0])
    precondition = jnp.dot(
        diag_own[...].T.astype(BF16), diag_other[...].astype(BF16), preferred_element_type=F32
    )
    stat_copy.wait_recv()
    sends_left = [stat_copy]
    total = stats[0] + stats_in[0]
    squared = total[0:1] + EPSILON
    inv = 1.0 / jnp.sqrt(squared)
    rayleigh = total[1:2] / squared
    vv = total[0:1] / squared
    vector = start * wide(inv)
    image = image * wide(inv)

    def correction_of(vector, image, rayleigh):
        shift = wide(rayleigh)
        return (image - shift * vector) / jnp.maximum(jnp.abs(precondition - shift), 1.0)

    raw = correction_of(vector, image, rayleigh)
    raw_image = apply_operator(raw)
    stats[1] = rows_of(vector * raw, raw * raw, vector * raw_image, raw * raw_image, raw * image)
    stat_copy = to_partner(stats.at[1], stats_in.at[1], stat_send.at[1], stat_recv.at[1])
    stat_copy.wait_recv()
    sends_left.append(stat_copy)
    total = stats[1] + stats_in[1]
    energy_one, scale_v, scale_c, rayleigh, vv = project(
        vv, rayleigh, *(total[q:q + 1] for q in range(5))
    )
    vector = wide(scale_v) * vector + wide(scale_c) * raw
    image = wide(scale_v) * image + wide(scale_c) * raw_image

    raw = correction_of(vector, image, rayleigh)
    raw_image = apply_operator(raw)
    sums = rows_of(vector * raw, raw * raw, vector * raw_image, raw * raw_image, raw * image)
    share = 0.5
    gathered[parity, bond] = jnp.concatenate(
        [sums[0:5], share * vv, share * rayleigh, share * energy_one], axis=0
    )

    def to_device(target, slot):
        return pltpu.make_async_remote_copy(
            src_ref=gathered.at[parity, bond], dst_ref=gathered.at[parity, bond],
            send_sem=all_send.at[slot], recv_sem=all_recv.at[me],
            device_id={"seg": target}, device_id_type=pl.DeviceIdType.MESH,
        )

    def from_device(source):
        return pltpu.make_async_remote_copy(
            src_ref=gathered.at[parity, bond],
            dst_ref=gathered.at[lax.rem(source, 2), lax.div(source, 2)],
            send_sem=all_send.at[0], recv_sem=all_recv.at[source],
            device_id={"seg": source}, device_id_type=pl.DeviceIdType.MESH,
        )

    first = to_device(partner, 0)
    first.start()
    last_sends = [first]
    for step in range(1, n // 2):
        for side in range(2):
            copy = to_device(lax.rem(2 * bond + 2 * step + side, n), 2 * step - 1 + side)
            copy.start()
            last_sends.append(copy)
    from_device(partner).wait_recv()
    total = gathered[0, bond] + gathered[1, bond]
    energy_two, scale_v, scale_c, _, _ = project(
        total[5:6], total[6:7], *(total[q:q + 1] for q in range(5))
    )
    final = (wide(scale_v * float(size)) * vector + wide(scale_c * float(size)) * raw)

    @pl.when(odd)
    def _():
        wave_ref[0, 0] = final.T

    @pl.when(jnp.logical_not(odd))
    def _():
        wave_ref[0, 0] = final

    lane = lax.broadcasted_iota(jnp.int32, (1, 128), 1)
    energies_ref[...] = jnp.where(lane == 0, total[7:8], energy_two)[:, 0:ITERS]

    for step in range(1, n // 2):
        for side in range(2):
            from_device(lax.rem(2 * bond + 2 * step + side, n)).wait_recv()
    bonds = n // 2
    sums = [gathered[0, :, q, :] + gathered[1, :, q, :] for q in range(8)]
    bond_energy, _, _, _, _ = project(sums[5], sums[6], *sums[0:5])
    place = lax.broadcasted_iota(jnp.int32, (bonds, 128), 0).astype(F32)
    weight = (1.0 + 2.0 * place / float(max(bonds - 1, 1))) / float(bonds)
    sweep_one = jnp.sum(weight * sums[7], axis=0, keepdims=True)
    sweep_two = jnp.sum(weight * bond_energy, axis=0, keepdims=True)
    sweep_ref[0] = sweep_one[0, 0]
    sweep_ref[1] = sweep_two[0, 0]

    for copy in sends_left + last_sends:
        copy.wait_send()
    for pair in sends:
        for copy in pair:
            copy.wait_send()


def per_device(n, psi_start, block_sizes, environment):
    channels, size = environment.shape[3], environment.shape[4]
    chunk = 2 if channels % 2 == 0 else 1
    chunks = channels // chunk
    padded = -(-channels // 16) * 16
    bonds = n // 2
    dma = pltpu.SemaphoreType.DMA
    return pl.pallas_call(
        functools.partial(kernel, n, chunk),
        out_shape=(
            jax.ShapeDtypeStruct(psi_start.shape, F32),
            jax.ShapeDtypeStruct((1, ITERS), F32),
            jax.ShapeDtypeStruct((ITERS,), F32),
        ),
        in_specs=[
            pl.BlockSpec(memory_space=pl.ANY),
            pl.BlockSpec(memory_space=pltpu.SMEM),
            pl.BlockSpec(memory_space=pl.ANY),
        ],
        out_specs=(
            pl.BlockSpec(memory_space=pltpu.VMEM),
            pl.BlockSpec(memory_space=pltpu.VMEM),
            pl.BlockSpec(memory_space=pltpu.SMEM),
        ),
        scratch_shapes=[
            pltpu.VMEM((size, size), F32),
            pltpu.VMEM((channels, size, size), BF16),
            pltpu.VMEM((channels, size, size), BF16),
            pltpu.VMEM((size, channels * size), BF16),
            pltpu.VMEM((size, size), F32),
            pltpu.VMEM((padded, size), F32),
            pltpu.VMEM((padded, size), F32),
            pltpu.VMEM((2, 8, 128), F32),
            pltpu.VMEM((2, 8, 128), F32),
            pltpu.VMEM((2, bonds, 8, 128), F32),
            dma,
            dma((chunks,)),
            dma((2 * chunks,)),
            dma((2 * chunks,)),
            dma((2,)),
            dma((2,)),
            dma((n,)),
            dma((n,)),
        ],
        compiler_params=pltpu.CompilerParams(
            collective_id=0, has_side_effects=True, vmem_limit_bytes=48 * 1024 * 1024
        ),
    )(psi_start, block_sizes, environment)


def solution(mesh):
    in_specs = (
        P(("groups", "seg"), None, None, None),
        P(("groups", "seg"), None, None),
        P(("groups", "seg"), None, None, None, None, None),
    )
    out_specs = (P(("groups", "seg"), None, None, None), P(("groups", "seg"), None), P("groups"))
    return jax.shard_map(
        functools.partial(per_device, mesh.shape["seg"]),
        mesh=mesh, in_specs=in_specs, out_specs=out_specs, check_vma=False,
    )
```

```python
import functools

import jax
import jax.numpy as jnp
from jax import lax
from jax.experimental import pallas as pl
from jax.experimental.pallas import tpu as pltpu
from jax.sharding import PartitionSpec as P

ITERS = 2
MARKS = (0, 10, 20, 28, 34)
EPSILON = 1e-06
F32 = jnp.float32
BF16 = jnp.bfloat16


def ritz_pair(rayleigh, coupling, curvature):
    half_gap = 0.5 * (rayleigh - curvature)
    energy_now = 0.5 * (rayleigh + curvature) - jnp.sqrt(half_gap * half_gap + coupling * coupling)
    weight_old = curvature - energy_now
    weight_new = -coupling
    length_pair = jnp.sqrt(weight_old * weight_old + weight_new * weight_new)
    return energy_now, weight_old / length_pair, weight_new / length_pair


def project(vv, rayleigh, vc, cc, vh, ch, ci):
    squared = jnp.maximum(cc - vc * vc * (2.0 - vv), 0.0)
    inv = 1.0 / jnp.sqrt(squared + EPSILON)
    coupling = (vh - vc * rayleigh) * inv
    mirrored = (ci - vc * rayleigh) * inv
    curvature = (ch - vc * (ci + vh) + vc * vc * rayleigh) * (inv * inv)
    energy, old, new = ritz_pair(rayleigh, coupling, curvature)
    scale_c = new * inv
    scale_v = old - scale_c * vc
    next_rayleigh = old * old * rayleigh + old * new * (coupling + mirrored) + new * new * curvature
    next_vv = scale_v * scale_v * vv + 2.0 * scale_v * scale_c * vc + scale_c * scale_c * cc
    return energy, scale_v, scale_c, next_rayleigh, next_vv


def rows_of(*fields):
    rows = []
    for field in fields:
        if field.shape[0] > 1:
            field = jnp.sum(field, axis=0, keepdims=True)
        half = field.shape[1] // 128
        total = field[:, :128]
        for part in range(1, half):
            total = total + field[:, part * 128:(part + 1) * 128]
        rows.append(total)
    rows.append(jnp.zeros((8 - len(rows), 128), F32))
    stacked = jnp.concatenate(rows, axis=0)
    return jnp.broadcast_to(jnp.sum(stacked, axis=1, keepdims=True), (8, 128))


def kernel(
    n, groups, psi_ref, sizes_ref, env_ref, wave_ref, energies_ref, sweep_ref,
    psi, own, other, parts, diag_own, diag_other, stats, stats_in, gathered,
    psi_sem, own_sem, send_sem, recv_sem, stat_send, stat_recv, all_send, all_recv,
):
    channels, size = own.shape[0], own.shape[1]
    half = size // 2
    me = lax.axis_index("seg")
    parity = lax.rem(me, 2)
    partner = me + 1 - 2 * parity
    bond = lax.div(me, 2)
    odd = parity == 1

    barrier = pltpu.get_barrier_semaphore()
    for step in range(1, n):
        pl.semaphore_signal(
            barrier, inc=1, device_id={"seg": lax.rem(me + step, n)}, device_id_type=pl.DeviceIdType.MESH
        )
    psi_copy = pltpu.make_async_copy(psi_ref.at[0, 0], psi, psi_sem)
    psi_copy.start()
    own_copies = []
    for g, (low, high) in enumerate(groups):
        ks = pl.ds(low, high - low)
        own_copies.append(pltpu.make_async_copy(env_ref.at[0, 0, 0, ks], own.at[ks], own_sem.at[g]))
        own_copies[-1].start()

    def to_partner(src, dst, sent, received):
        copy = pltpu.make_async_remote_copy(
            src_ref=src, dst_ref=dst, send_sem=sent, recv_sem=received,
            device_id={"seg": partner}, device_id_type=pl.DeviceIdType.MESH,
        )
        copy.start()
        return copy

    stat_copies = []

    def exchange(slot, sums):
        stats[slot] = sums
        copy = to_partner(stats.at[slot], stats_in.at[slot], stat_send.at[slot], stat_recv.at[slot])
        stat_copies.append(copy)
        return copy

    row_at = lax.broadcasted_iota(jnp.int32, (size, size), 0)
    col_at = lax.broadcasted_iota(jnp.int32, (size, size), 1)
    dim0, dim1 = sizes_ref[0, 0, 0], sizes_ref[0, 0, 1]
    row_size = jnp.where(odd, dim1, dim0)
    col_size = jnp.where(odd, dim0, dim1)

    def masked(field):
        return jnp.where((row_at < row_size) & (col_at < col_size), field, 0.0)

    def wide(row):
        return jnp.concatenate([row] * (size // 128), axis=1)

    eye = (
        lax.broadcasted_iota(jnp.int32, (half, half), 0) == lax.broadcasted_iota(jnp.int32, (half, half), 1)
    )

    def diagonals(ref, out, k):
        low = jnp.where(eye, ref[k, 0:half, 0:half].astype(F32), 0.0)
        high = jnp.where(eye, ref[k, half:size, half:size].astype(F32), 0.0)
        out[k:k + 1, 0:half] = jnp.sum(low, axis=0, keepdims=True)
        out[k:k + 1, half:size] = jnp.sum(high, axis=0, keepdims=True)

    def stage_one(low, first, last):
        products = jnp.dot(
            own[first:last].reshape((last - first) * size, size), low, preferred_element_type=F32
        ).astype(BF16)
        for k in range(first, last):
            parts[:, k * size:(k + 1) * size] = products[(k - first) * size:(k - first + 1) * size]

    def stage_two(first, last):
        return jnp.dot(
            parts[:, first * size:last * size],
            other[first:last].reshape((last - first) * size, size),
            preferred_element_type=F32,
        )

    psi_copy.wait()

    @pl.when(odd)
    def _():
        psi[...] = psi[...].T

    start = masked(psi[...])
    psi[...] = start
    sums = rows_of(start * start)
    pl.semaphore_wait(barrier, n - 1)

    norm_copy = exchange(0, sums)
    sends = []
    for g, (low, high) in enumerate(groups):
        ks = pl.ds(low, high - low)
        sends.append((
            to_partner(
                env_ref.at[0, 1, 0, ks, pl.ds(0, half)], other.at[ks, pl.ds(0, half)],
                send_sem.at[0, g], recv_sem.at[0, g],
            ),
            to_partner(
                env_ref.at[0, 1, 0, ks, pl.ds(half, half), pl.ds(half, half)],
                other.at[ks, pl.ds(half, half), pl.ds(half, half)],
                send_sem.at[1, g], recv_sem.at[1, g],
            ),
        ))
    diag_own[...] = jnp.zeros_like(diag_own)
    diag_other[...] = jnp.zeros_like(diag_other)
    for copy in own_copies:
        copy.wait()
    norm_copy.wait_recv()
    total = stats[0] + stats_in[0]
    squared = total[0:1] + EPSILON
    vv = total[0:1] / squared
    psi[...] = psi[...] * wide(1.0 / jnp.sqrt(squared))
    stage_one(psi[...].astype(BF16), 0, channels)
    for k in range(channels):
        diagonals(own, diag_own, k)

    image = None
    for (low, high), copies in zip(groups, sends):
        for copy in copies:
            copy.wait_recv()
        for k in range(low, high):
            other[k, half:size, 0:half] = other[k, 0:half, half:size].T
        product = stage_two(low, high)
        image = product if image is None else image + product

    def apply_operator(field):
        stage_one(field.astype(BF16), 0, channels)
        return masked(stage_two(0, channels))

    vector = psi[...]
    image = masked(image)
    rayleigh_copy = exchange(1, rows_of(vector * image))
    for k in range(channels):
        diagonals(other, diag_other, k)
    precondition = jnp.dot(
        diag_own[...].T.astype(BF16), diag_other[...].astype(BF16), preferred_element_type=F32
    )
    rayleigh_copy.wait_recv()
    rayleigh = stats[1, 0:1] + stats_in[1, 0:1]

    def correction_of(vector, image, rayleigh):
        shift = wide(rayleigh)
        return (image - shift * vector) / jnp.maximum(jnp.abs(precondition - shift), 1.0)

    raw = correction_of(vector, image, rayleigh)
    raw_image = apply_operator(raw)
    exchange(
        2, rows_of(vector * raw, raw * raw, vector * raw_image, raw * raw_image, raw * image)
    ).wait_recv()
    total = stats[2] + stats_in[2]
    energy_one, scale_v, scale_c, rayleigh, vv = project(
        vv, rayleigh, *(total[q:q + 1] for q in range(5))
    )
    vector = wide(scale_v) * vector + wide(scale_c) * raw
    image = wide(scale_v) * image + wide(scale_c) * raw_image

    raw = correction_of(vector, image, rayleigh)
    raw_image = apply_operator(raw)
    sums = rows_of(vector * raw, raw * raw, vector * raw_image, raw * raw_image, raw * image)
    share = 0.5
    gathered[parity, bond] = jnp.concatenate(
        [sums[0:5], share * vv, share * rayleigh, share * energy_one], axis=0
    )

    def to_device(target, slot):
        return pltpu.make_async_remote_copy(
            src_ref=gathered.at[parity, bond], dst_ref=gathered.at[parity, bond],
            send_sem=all_send.at[slot], recv_sem=all_recv.at[me],
            device_id={"seg": target}, device_id_type=pl.DeviceIdType.MESH,
        )

    def from_device(source):
        return pltpu.make_async_remote_copy(
            src_ref=gathered.at[parity, bond],
            dst_ref=gathered.at[lax.rem(source, 2), lax.div(source, 2)],
            send_sem=all_send.at[0], recv_sem=all_recv.at[source],
            device_id={"seg": source}, device_id_type=pl.DeviceIdType.MESH,
        )

    far_first = sorted(range(1, n // 2), key=lambda step: abs(step - n // 4))
    first = to_device(partner, 0)
    first.start()
    last_sends = [first]
    for step in far_first:
        for side in range(2):
            copy = to_device(lax.rem(2 * bond + 2 * step + side, n), 2 * step - 1 + side)
            copy.start()
            last_sends.append(copy)
    from_device(partner).wait_recv()
    total = gathered[0, bond] + gathered[1, bond]
    energy_two, scale_v, scale_c, _, _ = project(
        total[5:6], total[6:7], *(total[q:q + 1] for q in range(5))
    )
    final = (wide(scale_v * float(size)) * vector + wide(scale_c * float(size)) * raw)

    @pl.when(odd)
    def _():
        wave_ref[0, 0] = final.T

    @pl.when(jnp.logical_not(odd))
    def _():
        wave_ref[0, 0] = final

    lane = lax.broadcasted_iota(jnp.int32, (1, 128), 1)
    energies_ref[...] = jnp.where(lane == 0, total[7:8], energy_two)[:, 0:ITERS]

    for step in range(1, n // 2):
        for side in range(2):
            from_device(lax.rem(2 * bond + 2 * step + side, n)).wait_recv()
    bonds = n // 2
    sums = [gathered[0, :, q, :] + gathered[1, :, q, :] for q in range(8)]
    bond_energy, _, _, _, _ = project(sums[5], sums[6], *sums[0:5])
    place = lax.broadcasted_iota(jnp.int32, (bonds, 128), 0).astype(F32)
    weight = (1.0 + 2.0 * place / float(max(bonds - 1, 1))) / float(bonds)
    sweep_one = jnp.sum(weight * sums[7], axis=0, keepdims=True)
    sweep_two = jnp.sum(weight * bond_energy, axis=0, keepdims=True)
    sweep_ref[0] = sweep_one[0, 0]
    sweep_ref[1] = sweep_two[0, 0]

    for copy in stat_copies + last_sends:
        copy.wait_send()
    for pair in sends:
        for copy in pair:
            copy.wait_send()


def group_bounds(channels):
    marks = sorted({channels * m // 34 for m in MARKS})
    return list(zip(marks[:-1], marks[1:]))


def per_device(n, psi_start, block_sizes, environment):
    channels, size = environment.shape[3], environment.shape[4]
    groups = group_bounds(channels)
    chunks = len(groups)
    padded = -(-channels // 16) * 16
    bonds = n // 2
    dma = pltpu.SemaphoreType.DMA
    return pl.pallas_call(
        functools.partial(kernel, n, groups),
        out_shape=(
            jax.ShapeDtypeStruct(psi_start.shape, F32),
            jax.ShapeDtypeStruct((1, ITERS), F32),
            jax.ShapeDtypeStruct((ITERS,), F32),
        ),
        in_specs=[
            pl.BlockSpec(memory_space=pl.ANY),
            pl.BlockSpec(memory_space=pltpu.SMEM),
            pl.BlockSpec(memory_space=pl.ANY),
        ],
        out_specs=(
            pl.BlockSpec(memory_space=pltpu.VMEM),
            pl.BlockSpec(memory_space=pltpu.VMEM),
            pl.BlockSpec(memory_space=pltpu.SMEM),
        ),
        scratch_shapes=[
            pltpu.VMEM((size, size), F32),
            pltpu.VMEM((channels, size, size), BF16),
            pltpu.VMEM((channels, size, size), BF16),
            pltpu.VMEM((size, channels * size), BF16),
            pltpu.VMEM((padded, size), F32),
            pltpu.VMEM((padded, size), F32),
            pltpu.VMEM((3, 8, 128), F32),
            pltpu.VMEM((3, 8, 128), F32),
            pltpu.VMEM((2, bonds, 8, 128), F32),
            dma,
            dma((chunks,)),
            dma((2, chunks)),
            dma((2, chunks)),
            dma((3,)),
            dma((3,)),
            dma((n,)),
            dma((n,)),
        ],
        compiler_params=pltpu.CompilerParams(
            collective_id=0, has_side_effects=True, vmem_limit_bytes=48 * 1024 * 1024
        ),
    )(psi_start, block_sizes, environment)


def solution(mesh):
    in_specs = (
        P(("groups", "seg"), None, None, None),
        P(("groups", "seg"), None, None),
        P(("groups", "seg"), None, None, None, None, None),
    )
    out_specs = (P(("groups", "seg"), None, None, None), P(("groups", "seg"), None), P("groups"))
    return jax.shard_map(
        functools.partial(per_device, mesh.shape["seg"]),
        mesh=mesh, in_specs=in_specs, out_specs=out_specs, check_vma=False,
    )
```

```python
import functools

import jax
import jax.numpy as jnp
from jax import lax
from jax.experimental import pallas as pl
from jax.experimental.pallas import tpu as pltpu
from jax.sharding import PartitionSpec as P

ITERS = 2
MARKS = (0, 10, 20, 28, 34)
EPSILON = 1e-06
F32 = jnp.float32
BF16 = jnp.bfloat16


def ritz_pair(rayleigh, coupling, curvature):
    half_gap = 0.5 * (rayleigh - curvature)
    energy_now = 0.5 * (rayleigh + curvature) - jnp.sqrt(half_gap * half_gap + coupling * coupling)
    weight_old = curvature - energy_now
    weight_new = -coupling
    length_pair = jnp.sqrt(weight_old * weight_old + weight_new * weight_new)
    return energy_now, weight_old / length_pair, weight_new / length_pair


def project(vv, rayleigh, vc, cc, vh, ch, ci):
    squared = jnp.maximum(cc - vc * vc * (2.0 - vv), 0.0)
    inv = 1.0 / jnp.sqrt(squared + EPSILON)
    coupling = (vh - vc * rayleigh) * inv
    mirrored = (ci - vc * rayleigh) * inv
    curvature = (ch - vc * (ci + vh) + vc * vc * rayleigh) * (inv * inv)
    energy, old, new = ritz_pair(rayleigh, coupling, curvature)
    scale_c = new * inv
    scale_v = old - scale_c * vc
    next_rayleigh = old * old * rayleigh + old * new * (coupling + mirrored) + new * new * curvature
    next_vv = scale_v * scale_v * vv + 2.0 * scale_v * scale_c * vc + scale_c * scale_c * cc
    return energy, scale_v, scale_c, next_rayleigh, next_vv


def rows_of(*fields):
    rows = []
    for field in fields:
        if field.shape[0] > 1:
            field = jnp.sum(field, axis=0, keepdims=True)
        half = field.shape[1] // 128
        total = field[:, :128]
        for part in range(1, half):
            total = total + field[:, part * 128:(part + 1) * 128]
        rows.append(total)
    rows.append(jnp.zeros((8 - len(rows), 128), F32))
    stacked = jnp.concatenate(rows, axis=0)
    return jnp.broadcast_to(jnp.sum(stacked, axis=1, keepdims=True), (8, 128))


def kernel(
    n, groups, psi_ref, sizes_ref, env_ref, wave_ref, energies_ref, sweep_ref,
    psi, own, other, parts, diag_own, diag_other, stats, stats_in, gathered,
    psi_sem, own_sem, send_sem, recv_sem, stat_send, stat_recv, all_send, all_recv,
):
    channels, size = own.shape[0], own.shape[1]
    half = size // 2
    me = lax.axis_index("seg")
    parity = lax.rem(me, 2)
    partner = me + 1 - 2 * parity
    bond = lax.div(me, 2)
    odd = parity == 1

    barrier = pltpu.get_barrier_semaphore()
    for step in range(1, n):
        pl.semaphore_signal(
            barrier, inc=1, device_id={"seg": lax.rem(me + step, n)}, device_id_type=pl.DeviceIdType.MESH
        )
    psi_copy = pltpu.make_async_copy(psi_ref.at[0, 0], psi, psi_sem)
    psi_copy.start()
    own_copies = []
    for g, (low, high) in enumerate(groups):
        ks = pl.ds(low, high - low)
        own_copies.append(pltpu.make_async_copy(env_ref.at[0, 0, 0, ks], own.at[ks], own_sem.at[g]))
        own_copies[-1].start()

    def to_partner(src, dst, sent, received):
        copy = pltpu.make_async_remote_copy(
            src_ref=src, dst_ref=dst, send_sem=sent, recv_sem=received,
            device_id={"seg": partner}, device_id_type=pl.DeviceIdType.MESH,
        )
        copy.start()
        return copy

    stat_copies = []

    def exchange(slot, sums):
        stats[slot] = sums
        copy = to_partner(stats.at[slot], stats_in.at[slot], stat_send.at[slot], stat_recv.at[slot])
        stat_copies.append(copy)
        return copy

    row_at = lax.broadcasted_iota(jnp.int32, (size, size), 0)
    col_at = lax.broadcasted_iota(jnp.int32, (size, size), 1)
    dim0, dim1 = sizes_ref[0, 0, 0], sizes_ref[0, 0, 1]
    row_size = jnp.where(odd, dim1, dim0)
    col_size = jnp.where(odd, dim0, dim1)

    def masked(field):
        return jnp.where((row_at < row_size) & (col_at < col_size), field, 0.0)

    def wide(row):
        return jnp.concatenate([row] * (size // 128), axis=1)

    eye = (
        lax.broadcasted_iota(jnp.int32, (half, half), 0) == lax.broadcasted_iota(jnp.int32, (half, half), 1)
    )

    def diagonals(ref, out, k):
        low = jnp.where(eye, ref[k, 0:half, 0:half].astype(F32), 0.0)
        high = jnp.where(eye, ref[k, half:size, half:size].astype(F32), 0.0)
        out[k:k + 1, 0:half] = jnp.sum(low, axis=0, keepdims=True)
        out[k:k + 1, half:size] = jnp.sum(high, axis=0, keepdims=True)

    def stage_one(low, first, last):
        products = jnp.dot(
            own[first:last].reshape((last - first) * size, size), low, preferred_element_type=F32
        ).astype(BF16)
        for k in range(first, last):
            parts[:, k * size:(k + 1) * size] = products[(k - first) * size:(k - first + 1) * size]

    def stage_two(first, last):
        return jnp.dot(
            parts[:, first * size:last * size],
            other[first:last].reshape((last - first) * size, size),
            preferred_element_type=F32,
        )

    psi_copy.wait()

    @pl.when(odd)
    def _():
        psi[...] = psi[...].T

    start = masked(psi[...])
    psi[...] = start
    sums = rows_of(start * start)
    pl.semaphore_wait(barrier, n - 1)

    norm_copy = exchange(0, sums)
    sends = []
    for g, (low, high) in enumerate(groups):
        ks = pl.ds(low, high - low)
        sends.append((
            to_partner(
                env_ref.at[0, 1, 0, ks, pl.ds(0, half)], other.at[ks, pl.ds(0, half)],
                send_sem.at[0, g], recv_sem.at[0, g],
            ),
            to_partner(
                env_ref.at[0, 1, 0, ks, pl.ds(half, half), pl.ds(half, half)],
                other.at[ks, pl.ds(half, half), pl.ds(half, half)],
                send_sem.at[1, g], recv_sem.at[1, g],
            ),
        ))
    diag_own[...] = jnp.zeros_like(diag_own)
    diag_other[...] = jnp.zeros_like(diag_other)
    for copy in own_copies:
        copy.wait()
    norm_copy.wait_recv()
    total = stats[0] + stats_in[0]
    squared = total[0:1] + EPSILON
    vv = total[0:1] / squared
    psi[...] = psi[...] * wide(1.0 / jnp.sqrt(squared))
    stage_one(psi[...].astype(BF16), 0, channels)
    for k in range(channels):
        diagonals(own, diag_own, k)

    image = None
    for (low, high), copies in zip(groups, sends):
        for copy in copies:
            copy.wait_recv()
        for k in range(low, high):
            other[k, half:size, 0:half] = other[k, 0:half, half:size].T
        product = stage_two(low, high)
        image = product if image is None else image + product

    def apply_operator(field):
        stage_one(field.astype(BF16), 0, channels)
        return masked(stage_two(0, channels))

    vector = psi[...]
    image = masked(image)
    rayleigh_copy = exchange(1, rows_of(vector * image))
    for k in range(channels):
        diagonals(other, diag_other, k)
    precondition = jnp.dot(
        diag_own[...].T.astype(BF16), diag_other[...].astype(BF16), preferred_element_type=F32
    )
    rayleigh_copy.wait_recv()
    rayleigh = stats[1, 0:1] + stats_in[1, 0:1]

    def correction_of(vector, image, rayleigh):
        shift = wide(rayleigh)
        return (image - shift * vector) / jnp.maximum(jnp.abs(precondition - shift), 1.0)

    raw = correction_of(vector, image, rayleigh)
    raw_image = apply_operator(raw)
    exchange(
        2, rows_of(vector * raw, raw * raw, vector * raw_image, raw * raw_image, raw * image)
    ).wait_recv()
    total = stats[2] + stats_in[2]
    energy_one, scale_v, scale_c, rayleigh, vv = project(
        vv, rayleigh, *(total[q:q + 1] for q in range(5))
    )
    vector = wide(scale_v) * vector + wide(scale_c) * raw
    image = wide(scale_v) * image + wide(scale_c) * raw_image

    raw = correction_of(vector, image, rayleigh)
    raw_image = apply_operator(raw)
    sums = rows_of(vector * raw, raw * raw, vector * raw_image, raw * raw_image, raw * image)
    share = 0.5
    gathered[parity, bond] = jnp.concatenate(
        [sums[0:5], share * vv, share * rayleigh, share * energy_one], axis=0
    )

    def to_device(target, slot):
        return pltpu.make_async_remote_copy(
            src_ref=gathered.at[parity, bond], dst_ref=gathered.at[parity, bond],
            send_sem=all_send.at[slot], recv_sem=all_recv.at[me],
            device_id={"seg": target}, device_id_type=pl.DeviceIdType.MESH,
        )

    def from_device(source):
        return pltpu.make_async_remote_copy(
            src_ref=gathered.at[parity, bond],
            dst_ref=gathered.at[lax.rem(source, 2), lax.div(source, 2)],
            send_sem=all_send.at[0], recv_sem=all_recv.at[source],
            device_id={"seg": source}, device_id_type=pl.DeviceIdType.MESH,
        )

    far_first = sorted(range(1, n // 2), key=lambda step: abs(step - n // 4))
    first = to_device(partner, 0)
    first.start()
    last_sends = [first]
    for step in far_first:
        for side in range(2):
            copy = to_device(lax.rem(2 * bond + 2 * step + side, n), 2 * step - 1 + side)
            copy.start()
            last_sends.append(copy)
    from_device(partner).wait_recv()
    total = gathered[0, bond] + gathered[1, bond]
    energy_two, scale_v, scale_c, _, _ = project(
        total[5:6], total[6:7], *(total[q:q + 1] for q in range(5))
    )
    final = (wide(scale_v * float(size)) * vector + wide(scale_c * float(size)) * raw)

    @pl.when(odd)
    def _():
        psi[...] = final.T

    @pl.when(jnp.logical_not(odd))
    def _():
        psi[...] = final

    wave_copy = pltpu.make_async_copy(psi, wave_ref.at[0, 0], psi_sem)
    wave_copy.start()
    lane = lax.broadcasted_iota(jnp.int32, (1, 128), 1)
    energies_ref[...] = jnp.where(lane == 0, total[7:8], energy_two)[:, 0:ITERS]

    for step in range(1, n // 2):
        for side in range(2):
            from_device(lax.rem(2 * bond + 2 * step + side, n)).wait_recv()
    bonds = n // 2
    sums = [gathered[0, :, q, :] + gathered[1, :, q, :] for q in range(8)]
    bond_energy, _, _, _, _ = project(sums[5], sums[6], *sums[0:5])
    place = lax.broadcasted_iota(jnp.int32, (bonds, 128), 0).astype(F32)
    weight = (1.0 + 2.0 * place / float(max(bonds - 1, 1))) / float(bonds)
    sweep_one = jnp.sum(weight * sums[7], axis=0, keepdims=True)
    sweep_two = jnp.sum(weight * bond_energy, axis=0, keepdims=True)
    sweep_ref[0] = sweep_one[0, 0]
    sweep_ref[1] = sweep_two[0, 0]

    wave_copy.wait()
    for copy in stat_copies + last_sends:
        copy.wait_send()
    for pair in sends:
        for copy in pair:
            copy.wait_send()


def group_bounds(channels):
    marks = sorted({channels * m // 34 for m in MARKS})
    return list(zip(marks[:-1], marks[1:]))


def per_device(n, psi_start, block_sizes, environment):
    channels, size = environment.shape[3], environment.shape[4]
    groups = group_bounds(channels)
    chunks = len(groups)
    padded = -(-channels // 16) * 16
    bonds = n // 2
    dma = pltpu.SemaphoreType.DMA
    results = pl.pallas_call(
        functools.partial(kernel, n, groups),
        out_shape=(
            jax.ShapeDtypeStruct(psi_start.shape, F32),
            jax.ShapeDtypeStruct((1, ITERS), F32),
            jax.ShapeDtypeStruct((ITERS,), F32),
        ),
        in_specs=[
            pl.BlockSpec(memory_space=pl.ANY),
            pl.BlockSpec(memory_space=pltpu.SMEM),
            pl.BlockSpec(memory_space=pl.ANY),
        ],
        out_specs=(
            pl.BlockSpec(memory_space=pl.ANY),
            pl.BlockSpec(memory_space=pltpu.VMEM),
            pl.BlockSpec(memory_space=pltpu.SMEM),
        ),
        scratch_shapes=[
            pltpu.VMEM((size, size), F32),
            pltpu.VMEM((channels, size, size), BF16),
            pltpu.VMEM((channels, size, size), BF16),
            pltpu.VMEM((size, channels * size), BF16),
            pltpu.VMEM((padded, size), F32),
            pltpu.VMEM((padded, size), F32),
            pltpu.VMEM((3, 8, 128), F32),
            pltpu.VMEM((3, 8, 128), F32),
            pltpu.VMEM((2, bonds, 8, 128), F32),
            dma,
            dma((chunks,)),
            dma((2, chunks)),
            dma((2, chunks)),
            dma((3,)),
            dma((3,)),
            dma((n,)),
            dma((n,)),
        ],
        compiler_params=pltpu.CompilerParams(
            collective_id=0, has_side_effects=True, vmem_limit_bytes=60 * 1024 * 1024
        ),
    )(psi_start, block_sizes, environment)
    return pl.pallas_call(
        hand_over,
        out_shape=tuple(jax.ShapeDtypeStruct(r.shape, r.dtype) for r in results),
        in_specs=[pl.BlockSpec(memory_space=pltpu.VMEM)] * 3,
        out_specs=tuple([pl.BlockSpec(memory_space=pltpu.VMEM)] * 3),
    )(*results)


def hand_over(wave, energies, sweep, wave_out, energies_out, sweep_out):
    wave_out[...] = wave[...]
    energies_out[...] = energies[...]
    sweep_out[...] = sweep[...]


def solution(mesh):
    in_specs = (
        P(("groups", "seg"), None, None, None),
        P(("groups", "seg"), None, None),
        P(("groups", "seg"), None, None, None, None, None),
    )
    out_specs = (P(("groups", "seg"), None, None, None), P(("groups", "seg"), None), P("groups"))
    return jax.shard_map(
        functools.partial(per_device, mesh.shape["seg"]),
        mesh=mesh, in_specs=in_specs, out_specs=out_specs, check_vma=False,
    )
```

```python
import functools

import jax
import jax.numpy as jnp
from jax import lax
from jax.experimental import pallas as pl
from jax.experimental.pallas import tpu as pltpu
from jax.sharding import PartitionSpec as P

ITERS = 2
MARKS = (0, 10, 20, 28, 34)
EPSILON = 1e-06
F32 = jnp.float32
BF16 = jnp.bfloat16


def ritz_pair(rayleigh, coupling, curvature):
    half_gap = 0.5 * (rayleigh - curvature)
    energy_now = 0.5 * (rayleigh + curvature) - jnp.sqrt(half_gap * half_gap + coupling * coupling)
    weight_old = curvature - energy_now
    weight_new = -coupling
    length_pair = jnp.sqrt(weight_old * weight_old + weight_new * weight_new)
    return energy_now, weight_old / length_pair, weight_new / length_pair


def project(vv, rayleigh, vc, cc, vh, ch, ci):
    squared = jnp.maximum(cc - vc * vc * (2.0 - vv), 0.0)
    inv = 1.0 / jnp.sqrt(squared + EPSILON)
    coupling = (vh - vc * rayleigh) * inv
    mirrored = (ci - vc * rayleigh) * inv
    curvature = (ch - vc * (ci + vh) + vc * vc * rayleigh) * (inv * inv)
    energy, old, new = ritz_pair(rayleigh, coupling, curvature)
    scale_c = new * inv
    scale_v = old - scale_c * vc
    next_rayleigh = old * old * rayleigh + old * new * (coupling + mirrored) + new * new * curvature
    next_vv = scale_v * scale_v * vv + 2.0 * scale_v * scale_c * vc + scale_c * scale_c * cc
    return energy, scale_v, scale_c, next_rayleigh, next_vv


def rows_of(*fields):
    rows = []
    for field in fields:
        if field.shape[0] > 1:
            field = jnp.sum(field, axis=0, keepdims=True)
        half = field.shape[1] // 128
        total = field[:, :128]
        for part in range(1, half):
            total = total + field[:, part * 128:(part + 1) * 128]
        rows.append(total)
    rows.append(jnp.zeros((8 - len(rows), 128), F32))
    stacked = jnp.concatenate(rows, axis=0)
    return jnp.broadcast_to(jnp.sum(stacked, axis=1, keepdims=True), (8, 128))


def kernel(
    n, groups, psi_ref, sizes_ref, env_ref, wave_ref, energies_ref, sweep_ref,
    psi, own, other, parts, diag_own, diag_other, stats, stats_in, gathered,
    psi_sem, own_sem, send_sem, recv_sem, stat_send, stat_recv, all_send, all_recv,
):
    channels, size = own.shape[0], own.shape[1]
    half = size // 2
    me = lax.axis_index("seg")
    parity = lax.rem(me, 2)
    partner = me + 1 - 2 * parity
    bond = lax.div(me, 2)
    odd = parity == 1

    barrier = pltpu.get_barrier_semaphore()
    for step in range(1, n):
        pl.semaphore_signal(
            barrier, inc=1, device_id={"seg": lax.rem(me + step, n)}, device_id_type=pl.DeviceIdType.MESH
        )
    psi_copy = pltpu.make_async_copy(psi_ref.at[0, 0], psi, psi_sem)
    psi_copy.start()
    own_copies = []
    for g, (low, high) in enumerate(groups):
        ks = pl.ds(low, high - low)
        own_copies.append(pltpu.make_async_copy(env_ref.at[0, 0, 0, ks], own.at[ks], own_sem.at[g]))
        own_copies[-1].start()

    def to_partner(src, dst, sent, received):
        copy = pltpu.make_async_remote_copy(
            src_ref=src, dst_ref=dst, send_sem=sent, recv_sem=received,
            device_id={"seg": partner}, device_id_type=pl.DeviceIdType.MESH,
        )
        copy.start()
        return copy

    stat_copies = []

    def exchange(slot, sums):
        stats[slot] = sums
        copy = to_partner(stats.at[slot], stats_in.at[slot], stat_send.at[slot], stat_recv.at[slot])
        stat_copies.append(copy)
        return copy

    row_at = lax.broadcasted_iota(jnp.int32, (size, size), 0)
    col_at = lax.broadcasted_iota(jnp.int32, (size, size), 1)
    dim0, dim1 = sizes_ref[0, 0, 0], sizes_ref[0, 0, 1]
    row_size = jnp.where(odd, dim1, dim0)
    col_size = jnp.where(odd, dim0, dim1)

    def masked(field):
        return jnp.where((row_at < row_size) & (col_at < col_size), field, 0.0)

    def wide(row):
        return jnp.concatenate([row] * (size // 128), axis=1)

    eye = (
        lax.broadcasted_iota(jnp.int32, (half, half), 0) == lax.broadcasted_iota(jnp.int32, (half, half), 1)
    )

    def diagonals(ref, out, k):
        low = jnp.where(eye, ref[k, 0:half, 0:half].astype(F32), 0.0)
        high = jnp.where(eye, ref[k, half:size, half:size].astype(F32), 0.0)
        out[k:k + 1, 0:half] = jnp.sum(low, axis=0, keepdims=True)
        out[k:k + 1, half:size] = jnp.sum(high, axis=0, keepdims=True)

    def stage_one(low, first, last):
        products = jnp.dot(
            own[first:last].reshape((last - first) * size, size), low, preferred_element_type=F32
        ).astype(BF16)
        for k in range(first, last):
            parts[:, k * size:(k + 1) * size] = products[(k - first) * size:(k - first + 1) * size]

    def stage_two(first, last):
        return jnp.dot(
            parts[:, first * size:last * size],
            other[first:last].reshape((last - first) * size, size),
            preferred_element_type=F32,
        )

    psi_copy.wait()

    @pl.when(odd)
    def _():
        psi[...] = psi[...].T

    start = masked(psi[...])
    psi[...] = start
    sums = rows_of(start * start)
    pl.semaphore_wait(barrier, n - 1)

    norm_copy = exchange(0, sums)
    sends = []
    for g, (low, high) in enumerate(groups):
        ks = pl.ds(low, high - low)
        sends.append((
            to_partner(
                env_ref.at[0, 1, 0, ks, pl.ds(0, half)], other.at[ks, pl.ds(0, half)],
                send_sem.at[0, g], recv_sem.at[0, g],
            ),
            to_partner(
                env_ref.at[0, 1, 0, ks, pl.ds(half, half), pl.ds(half, half)],
                other.at[ks, pl.ds(half, half), pl.ds(half, half)],
                send_sem.at[1, g], recv_sem.at[1, g],
            ),
        ))
    diag_own[...] = jnp.zeros_like(diag_own)
    diag_other[...] = jnp.zeros_like(diag_other)
    for copy in own_copies:
        copy.wait()
    norm_copy.wait_recv()
    total = stats[0] + stats_in[0]
    squared = total[0:1] + EPSILON
    vv = total[0:1] / squared
    psi[...] = psi[...] * wide(1.0 / jnp.sqrt(squared))
    stage_one(psi[...].astype(BF16), 0, channels)
    image = None
    for (low, high), copies in zip(groups, sends):
        for copy in copies:
            copy.wait_recv()
        for k in range(low, high):
            other[k, half:size, 0:half] = other[k, 0:half, half:size].T
        product = stage_two(low, high)
        image = product if image is None else image + product

    def apply_operator(field):
        products = jnp.dot(
            own[...].reshape(channels * size, size), field.astype(BF16), preferred_element_type=F32
        ).astype(BF16)
        joined = jnp.concatenate([products[k * size:(k + 1) * size] for k in range(channels)], axis=1)
        return masked(jnp.dot(
            joined, other[...].reshape(channels * size, size), preferred_element_type=F32
        ))

    vector = psi[...]
    image = masked(image)
    rayleigh_copy = exchange(1, rows_of(vector * image))
    for k in range(channels):
        diagonals(own, diag_own, k)
        diagonals(other, diag_other, k)
    precondition = jnp.dot(
        diag_own[...].T.astype(BF16), diag_other[...].astype(BF16), preferred_element_type=F32
    )
    rayleigh_copy.wait_recv()
    rayleigh = stats[1, 0:1] + stats_in[1, 0:1]

    def correction_of(vector, image, rayleigh):
        shift = wide(rayleigh)
        return (image - shift * vector) / jnp.maximum(jnp.abs(precondition - shift), 1.0)

    raw = correction_of(vector, image, rayleigh)
    raw_image = apply_operator(raw)
    exchange(
        2, rows_of(vector * raw, raw * raw, vector * raw_image, raw * raw_image, raw * image)
    ).wait_recv()
    total = stats[2] + stats_in[2]
    energy_one, scale_v, scale_c, rayleigh, vv = project(
        vv, rayleigh, *(total[q:q + 1] for q in range(5))
    )
    vector = wide(scale_v) * vector + wide(scale_c) * raw
    image = wide(scale_v) * image + wide(scale_c) * raw_image

    raw = correction_of(vector, image, rayleigh)
    raw_image = apply_operator(raw)
    sums = rows_of(vector * raw, raw * raw, vector * raw_image, raw * raw_image, raw * image)
    share = 0.5
    gathered[parity, bond] = jnp.concatenate(
        [sums[0:5], share * vv, share * rayleigh, share * energy_one], axis=0
    )

    def to_device(target, slot):
        return pltpu.make_async_remote_copy(
            src_ref=gathered.at[parity, bond], dst_ref=gathered.at[parity, bond],
            send_sem=all_send.at[slot], recv_sem=all_recv.at[me],
            device_id={"seg": target}, device_id_type=pl.DeviceIdType.MESH,
        )

    def from_device(source):
        return pltpu.make_async_remote_copy(
            src_ref=gathered.at[parity, bond],
            dst_ref=gathered.at[lax.rem(source, 2), lax.div(source, 2)],
            send_sem=all_send.at[0], recv_sem=all_recv.at[source],
            device_id={"seg": source}, device_id_type=pl.DeviceIdType.MESH,
        )

    far_first = sorted(range(1, n // 2), key=lambda step: abs(step - n // 4))
    first = to_device(partner, 0)
    first.start()
    last_sends = [first]
    for step in far_first:
        for side in range(2):
            copy = to_device(lax.rem(2 * bond + 2 * step + side, n), 2 * step - 1 + side)
            copy.start()
            last_sends.append(copy)
    from_device(partner).wait_recv()
    total = gathered[0, bond] + gathered[1, bond]
    energy_two, scale_v, scale_c, _, _ = project(
        total[5:6], total[6:7], *(total[q:q + 1] for q in range(5))
    )
    final = (wide(scale_v * float(size)) * vector + wide(scale_c * float(size)) * raw)

    @pl.when(odd)
    def _():
        psi[...] = final.T

    @pl.when(jnp.logical_not(odd))
    def _():
        psi[...] = final

    wave_copy = pltpu.make_async_copy(psi, wave_ref.at[0, 0], psi_sem)
    wave_copy.start()
    lane = lax.broadcasted_iota(jnp.int32, (1, 128), 1)
    energies_ref[...] = jnp.where(lane == 0, total[7:8], energy_two)[:, 0:ITERS]

    for step in range(1, n // 2):
        for side in range(2):
            from_device(lax.rem(2 * bond + 2 * step + side, n)).wait_recv()
    bonds = n // 2
    sums = [gathered[0, :, q, :] + gathered[1, :, q, :] for q in range(8)]
    bond_energy, _, _, _, _ = project(sums[5], sums[6], *sums[0:5])
    place = lax.broadcasted_iota(jnp.int32, (bonds, 128), 0).astype(F32)
    weight = (1.0 + 2.0 * place / float(max(bonds - 1, 1))) / float(bonds)
    sweep_one = jnp.sum(weight * sums[7], axis=0, keepdims=True)
    sweep_two = jnp.sum(weight * bond_energy, axis=0, keepdims=True)
    sweep_ref[0] = sweep_one[0, 0]
    sweep_ref[1] = sweep_two[0, 0]

    wave_copy.wait()
    for copy in stat_copies + last_sends:
        copy.wait_send()
    for pair in sends:
        for copy in pair:
            copy.wait_send()


def group_bounds(channels):
    marks = sorted({channels * m // 34 for m in MARKS})
    return list(zip(marks[:-1], marks[1:]))


def per_device(n, psi_start, block_sizes, environment):
    channels, size = environment.shape[3], environment.shape[4]
    groups = group_bounds(channels)
    chunks = len(groups)
    padded = -(-channels // 16) * 16
    bonds = n // 2
    dma = pltpu.SemaphoreType.DMA
    results = pl.pallas_call(
        functools.partial(kernel, n, groups),
        out_shape=(
            jax.ShapeDtypeStruct(psi_start.shape, F32),
            jax.ShapeDtypeStruct((1, ITERS), F32),
            jax.ShapeDtypeStruct((ITERS,), F32),
        ),
        in_specs=[
            pl.BlockSpec(memory_space=pl.ANY),
            pl.BlockSpec(memory_space=pltpu.SMEM),
            pl.BlockSpec(memory_space=pl.ANY),
        ],
        out_specs=(
            pl.BlockSpec(memory_space=pl.ANY),
            pl.BlockSpec(memory_space=pltpu.VMEM),
            pl.BlockSpec(memory_space=pltpu.SMEM),
        ),
        scratch_shapes=[
            pltpu.VMEM((size, size), F32),
            pltpu.VMEM((channels, size, size), BF16),
            pltpu.VMEM((channels, size, size), BF16),
            pltpu.VMEM((size, channels * size), BF16),
            pltpu.VMEM((padded, size), F32),
            pltpu.VMEM((padded, size), F32),
            pltpu.VMEM((3, 8, 128), F32),
            pltpu.VMEM((3, 8, 128), F32),
            pltpu.VMEM((2, bonds, 8, 128), F32),
            dma,
            dma((chunks,)),
            dma((2, chunks)),
            dma((2, chunks)),
            dma((3,)),
            dma((3,)),
            dma((n,)),
            dma((n,)),
        ],
        compiler_params=pltpu.CompilerParams(
            collective_id=0, has_side_effects=True, vmem_limit_bytes=60 * 1024 * 1024
        ),
    )(psi_start, block_sizes, environment)
    return pl.pallas_call(
        hand_over,
        out_shape=tuple(jax.ShapeDtypeStruct(r.shape, r.dtype) for r in results),
        in_specs=[pl.BlockSpec(memory_space=pltpu.VMEM)] * 3,
        out_specs=tuple([pl.BlockSpec(memory_space=pltpu.VMEM)] * 3),
    )(*results)


def hand_over(wave, energies, sweep, wave_out, energies_out, sweep_out):
    wave_out[...] = wave[...]
    energies_out[...] = energies[...]
    sweep_out[...] = sweep[...]


def solution(mesh):
    in_specs = (
        P(("groups", "seg"), None, None, None),
        P(("groups", "seg"), None, None),
        P(("groups", "seg"), None, None, None, None, None),
    )
    out_specs = (P(("groups", "seg"), None, None, None), P(("groups", "seg"), None), P("groups"))
    return jax.shard_map(
        functools.partial(per_device, mesh.shape["seg"]),
        mesh=mesh, in_specs=in_specs, out_specs=out_specs, check_vma=False,
    )
```
